128 devices in a mesh: blk: 16 (over z_lo, x, core), enc: 8 (over y, z_hi).
Axes of the slice: x: 4, y: 4, z: 4 (z_hi: 2, z_lo: 2; z = z_hi * 2 + z_lo), core: 2. Of those that a mesh axis runs over, the one named last changes fastest.
Arguments:
- queries: bfloat16 [128, 512, 128], P(('blk', 'enc')), may hold values from -6 to 6
- documents: bfloat16 [64, 1024, 128], P('blk'), may hold values from -6 to 6
- candidates: int32 [64, 8, 8], P('blk', 'enc'), may hold values from 0 to 15, all different within a row
- positions: int32 [64, 8, 8, 8, 512], P('blk', 'enc'), may hold values from 0 to 127
- labels: int32 [64, 8, 8, 8, 16], P('blk', 'enc'), may hold values 0 or 1
- owner_map: int32 [512, 1], P('blk'), may hold values from 0 to 7; in each aligned block of 32 rows (0 to 31, 32 to 63, ...) at most 8 rows name the same one
- hidden: bfloat16 [1024, 128, 768], P(('blk', 'enc')), may hold values from -0.005859375 to 0.005859375
- projection: bfloat16 [768, 128], replicated, may hold values from -0.21875 to 0.21875
Outputs:
- query_grad: float32 [128, 512, 128], P(('blk', 'enc'))
- hidden_grad: bfloat16 [1024, 128, 768], P(('blk', 'enc'))
- weight_grad: float32 [768, 128], replicated
The draws below stay inside these ranges and needn't reach their ends.
Inputs may be any that keep to these rules, and one draw needn't show every extreme that they name: `candidates`: each row names 8 different blk positions, and every position is named by some row. `owner_map`: in each shard of 32 documents no owner holds more than 8 documents, and in some shard one owner holds exactly 8.
All inputs are finite; a program needn't handle non-finite values. No bound on the sum of `labels` on one device may be relied on, other than what follows from the above.
Results may differ from the reference program's by a relative error of at most 0.014.
Values may be sent and summed in bfloat16 or wider, within the bound.
No kernel may reach another device: no remote copies, remote signals or barrier semaphores. Data moves between devices by JAX's collectives and lax.ppermute only.
A program may use at most 192 MiB of HBM per device.

```python
import math
import jax
import jax.numpy as jnp
import numpy as np
from jax import lax

DIM = 128
HID = 768
QT = 32
LD = 128
DB = 8
KQ = 8
QB = 16
DOC_SH = 32
QTOK = 512
CAP = 8
NDB = 64
DOCS = 512
NQB = 128
SLOTS = 1024
N_BLK = 16
N_ENC = 8


def place_ends(result, key, low, largest):
    longest = result.shape.index(max(result.shape))
    spots = []
    for shift in (0, 1):
        where = [jax.random.randint(jax.random.fold_in(key, axis), (), 0, length) for axis, length in enumerate(result.shape)]
        where[longest] = (where[longest] + shift) % result.shape[longest]
        spots.append(tuple(where))
    return result.at[spots[0]].set(low).at[spots[1]].set(largest)


def block_scale(rng, dims, shards, smallest, high):
    def one(position, blocks):
        steps = jax.random.uniform(jax.random.fold_in(jax.random.fold_in(rng, 6), position), (blocks,), jnp.float32, smallest / len(shards), high / len(shards))
        return jnp.repeat(jnp.exp(steps), dims[position] // blocks).reshape((-1,) + (1,) * (len(dims) - position - 1))

    gain = one(*shards[0])
    for cut in shards[1:]:
        gain = gain * one(*cut)
    return gain


def picks_of(rng, rows, amount, top, lift):
    order = jax.random.permutation(jax.random.fold_in(rng, 1), amount)
    pull = order
    for power in range(3):
        pull = pull * pull // amount
    pull = pull * lift // amount
    chance = jax.random.randint(jax.random.fold_in(rng, 2), (rows, amount), 0, 4096) + pull
    fixed_rows = jax.random.permutation(jax.random.fold_in(rng, 3), rows)[jnp.arange(amount) % rows]
    chance = jnp.where(jnp.arange(rows)[:, None] == fixed_rows[None, :], 1 << 14, chance)
    score = chance * amount + jnp.arange(amount)
    return lax.top_k(score.astype(jnp.int32), top)[1].astype(jnp.int32)


def shared_out(own_key, own, number, rows, amount, top, bound, skew):
    order = jax.random.permutation(own_key, amount)
    crowded, usual = load_shares(amount, rows * top, bound, skew, True), load_shares(amount, rows * top, bound, skew, False)
    places = jnp.arange(amount)

    def named(tallies, rotation):
        used = int((tallies > 0).sum())
        fixed = max(1, used // 4)
        passed = fixed + (places - fixed + rotation * (used - fixed)) % max(1, amount - fixed)
        return jnp.zeros((amount,), jnp.int32).at[order[jnp.where(places < fixed, places, passed)]].set(jnp.asarray(tallies, jnp.int32))

    tallies = jnp.where(number % 4 == 0, named(crowded, number // 4), named(usual, number - number // 4 - 1))
    mixed = jax.random.permutation(jax.random.fold_in(own, 3), amount)
    giver, sink = mixed[0:amount // 2 * 2:2], mixed[1:amount // 2 * 2:2]
    margin = jnp.minimum(tallies[giver] - 1, bound - tallies[sink]) // 2
    margin = jnp.where((giver == order[0]) | (sink == order[0]) | (tallies[sink] == 0), 0, jnp.maximum(margin, 0))
    passed = jax.random.randint(jax.random.fold_in(own, 4), (amount // 2,), 0, 1 << 20) % (margin + 1)
    tallies = tallies.at[giver].add(-passed).at[sink].add(passed)
    members = jnp.searchsorted(jnp.cumsum(tallies), jnp.arange(rows * top), side="right").astype(jnp.int32)
    listing = members.reshape(top, rows).T
    listing = listing[jax.random.permutation(jax.random.fold_in(own, 1), rows)]
    rotation = jax.random.randint(jax.random.fold_in(own, 2), (rows, 1), 0, top)
    return jnp.take_along_axis(listing, (jnp.arange(top)[None, :] + rotation) % top, axis=1)


def load_shares(number_of, total, most, skew, full):
    loads = [(1 << 20) // math.isqrt(standing ** skew) + 1 for standing in range(1, number_of + 1)]
    largest = most if full else min(most, max(-(-total // number_of), total * loads[0] // sum(loads)))
    least = 1 if total - largest >= number_of - 1 else 0
    counts, surplus = [largest] + [least] * (number_of - 1), total - largest - least * (number_of - 1)
    while surplus > 0:
        free = [i for i in range(1, number_of) if counts[i] < largest] or [i for i in range(1, number_of) if counts[i] < most]
        pool, budget = sum([loads[i] for i in free]), surplus
        for i in free:
            addition = min(most - counts[i], max(1, budget * loads[i] // pool), surplus)
            counts[i] = counts[i] + addition
            surplus = surplus - addition
    return np.array(counts)


def noise(rng, extent, scale, most, pieces=(), kind=jnp.bfloat16):
    array = jax.random.normal(rng, extent, jnp.float32) * scale
    if len(pieces) > 0:
        array = block_scale(rng, extent, pieces, -0.22, 0.18) * array
    return jnp.clip(array, min=-most, max=most).astype(kind)


def setup_inputs(seed: int = 0) -> dict:
    keys = jax.random.split(jax.random.key(seed), 9)
    queries = noise(keys[0], (NQB, QTOK, DIM), 1.0, 6.0, ((0, 128),))
    documents = noise(keys[1], (NDB, DB * LD, DIM), 1.0, 6.0, ((0, 16),))
    candidates = picks_of(keys[2], NDB * N_ENC, N_BLK, KQ, 8192).reshape((NDB, N_ENC, KQ))
    positions = place_ends(jax.random.randint(keys[3], (NDB, N_ENC, KQ, DB, QTOK), 0, LD), jax.random.fold_in(keys[3], 1), 0, LD - 1).astype(jnp.int32)
    labels = place_ends((jax.random.randint(keys[4], (NDB, N_ENC, KQ, DB, QB), 0, 4) < 1).astype(jnp.int32), jax.random.fold_in(keys[4], 1), 0, 1)
    owner_map_keys = jax.random.split(jax.random.fold_in(keys[5], 1), DOCS // DOC_SH)
    owner_map_turns = jax.random.permutation(jax.random.fold_in(keys[5], 3), DOCS // DOC_SH)
    owner_map = jax.vmap(lambda own, number: shared_out(jax.random.fold_in(keys[5], 2), own, number, DOC_SH, N_ENC, 1, CAP, 2))(owner_map_keys, owner_map_turns).reshape((DOCS, 1))
    hidden = noise(keys[6], (SLOTS, LD, HID), (16 * DOCS * LD) ** -0.5, 0.005859375, ((0, 128),))
    projection = noise(keys[7], (HID, DIM), HID ** -0.5, 0.21875)
    return {"queries": queries, "documents": documents, "candidates": candidates, "positions": positions, "labels": labels, "owner_map": owner_map, "hidden": hidden, "projection": projection}


def reference(queries, documents, candidates, positions, labels, owner_map, hidden, projection):
    factor = 1.0 / math.sqrt(QT * DIM)
    column = jnp.arange(N_ENC, dtype=jnp.int32)[:, None]
    offsets = (jnp.arange(DB, dtype=jnp.int32) * LD)[None, None, :, None]

    def per_block(query_sums, inputs):
        doc_block, picks, spots, marks = inputs
        block_ids = (picks * N_ENC + column).astype(jnp.int32)
        chosen_queries = queries[block_ids].astype(jnp.float32)
        rows_used = (offsets + spots).astype(jnp.int32)
        chosen_docs = doc_block[rows_used].astype(jnp.float32)
        score = jnp.einsum('ekud,ekrud->ekru', chosen_queries, chosen_docs)
        score = score.reshape(N_ENC, KQ, DB, QB, QT).sum(axis=-1)
        slope = (jax.nn.sigmoid(score * factor) - marks.astype(jnp.float32)).astype(jnp.bfloat16)
        spread = jnp.repeat(slope.astype(jnp.float32), QT, axis=-1)
        query_sums = query_sums.at[block_ids].add(jnp.einsum('ekru,ekrud->ekud', spread, chosen_docs))
        terms = spread[..., None] * chosen_queries[:, :, None]
        doc_part = jax.ops.segment_sum(terms.reshape(-1, DIM), rows_used.reshape(-1), num_segments=DB * LD)
        return (query_sums, doc_part)
    start = jnp.zeros((NQB, QB * QT, DIM), jnp.float32)
    query_grad, doc_sum = lax.scan(per_block, start, (documents, candidates, positions, labels))
    doc_grad = doc_sum.reshape(DOCS, LD, DIM).astype(jnp.bfloat16)
    owners = owner_map[:, 0].reshape(N_BLK, DOC_SH)
    marked = (owners[..., None] == jnp.arange(N_ENC, dtype=jnp.int32)).astype(jnp.int32)
    rank = lax.optimization_barrier(jnp.sum((jnp.cumsum(marked, axis=1) - marked) * marked, axis=-1))
    shard = jnp.arange(N_BLK, dtype=jnp.int32)[:, None]
    slot_rows = ((shard * N_ENC + owners) * CAP + rank).reshape(-1).astype(jnp.int32)
    slot_grad = jnp.zeros((SLOTS, LD, DIM), jnp.bfloat16).at[slot_rows].set(doc_grad)
    flat_grad = slot_grad.reshape(-1, DIM)
    flat_hidden = hidden.reshape(-1, HID)
    weight_grad = jnp.dot(flat_hidden.T, flat_grad, preferred_element_type=jnp.float32)
    hidden_grad = jnp.dot(flat_grad, projection.T, preferred_element_type=jnp.float32).astype(jnp.bfloat16)
    return (query_grad, hidden_grad.reshape(SLOTS, LD, HID), weight_grad)
```

```python
import functools
import math

import jax
import jax.numpy as jnp
from jax import lax
from jax.experimental import pallas as pl
from jax.experimental.pallas import tpu as pltpu
from jax.sharding import PartitionSpec as P

DIM = 128
QT = 32
LD = 128
DB = 8
KQ = 8
QB = 16
QTOK = 512
CAP = 8
NLOC = 4
N_BLK = 16
N_ENC = 8
BF = jnp.bfloat16
F32 = jnp.float32
NN = (((1,), (0,)), ((), ()))
NT = (((1,), (1,)), ((), ()))
BOTH = ("blk", "enc")


def coords(i):
    blk, enc = divmod(i, N_ENC)
    return blk >> 3, (blk >> 1) & 3, blk & 1, enc >> 1, enc & 1


def number(zl, x, c, y, zh):
    return (zl * 8 + x * 2 + c) * N_ENC + y * 2 + zh


def shift(value, zl=0, x=0, c=0, y=0, zh=0):
    pairs = []
    for i in range(N_BLK * N_ENC):
        a, b, d, e, f = coords(i)
        pairs.append((i, number(a ^ zl, (b + x) % 4, d ^ c, (e + y) % 4, f ^ zh)))
    return lax.ppermute(value, BOTH, pairs)


def dot(a, b, dims):
    return lax.dot_general(a, b, dims, preferred_element_type=F32)


def tile_body(
    place, cand, owners, docs, pos, lab, *refs
):
    qs = refs[:16]
    far, near = refs[16:18]
    outs = refs[18:22]
    q, qacc, dacc, docs_t, labs, w, dgrad, source, sems = refs[22:]
    copies = [pltpu.make_async_copy(qs[i], q.at[i], sems.at[i]) for i in range(16)]
    for copy in copies:
        copy.start()
    qacc[...] = jnp.zeros_like(qacc)
    my_zl, my_x, my_c = place[0] // 8, (place[0] // 2) % 4, place[0] % 2
    my_y, my_zh = place[1] // 2, place[1] % 2

    def clear(i, _):
        source[i] = -1
        return 0

    lax.fori_loop(0, N_ENC * CAP, clear, 0)

    def slot_of(i, _):
        o = owners[i]
        row = (((o // 2) - my_y + 4) % 4) * 2 + (o % 2 + my_zh) % 2
        def count(j, n):
            return n + jnp.where(owners[j] == o, 1, 0)
        rank = lax.fori_loop(0, i, count, 0)
        source[row * CAP + rank] = i
        return 0

    lax.fori_loop(0, NLOC * DB, slot_of, 0)

    i16 = lax.broadcasted_iota(jnp.int32, (16, QTOK), 0)
    i128 = lax.broadcasted_iota(jnp.int32, (LD, QTOK), 0)
    same = (
        lax.broadcasted_iota(jnp.int32, (128, 128), 0) // QT
        == lax.broadcasted_iota(jnp.int32, (128, 128), 1) // QT
    ).astype(BF)
    spread = (
        lax.broadcasted_iota(jnp.int32, (QB, QTOK), 0)
        == lax.broadcasted_iota(jnp.int32, (QB, QTOK), 1) // QT
    ).astype(BF)
    labs[...] = dot(lab[...].astype(BF), spread, NN).reshape(labs.shape)
    for copy in copies:
        copy.wait()

    def per_c(c, _):
        docs_t[...] = docs[c].T
        dacc[...] = jnp.zeros_like(dacc)

        def per_k(k, _):
            t = c * KQ + k
            g = cand[t]
            rel = ((g + my_c) % 2) * 8 + ((g // 8 + my_zl) % 2) * 4 + ((g // 2) % 4 - my_x + 4) % 4
            block = q[rel]
            parts = []
            for r in range(DB):
                s = dot(docs[c, r * LD : (r + 1) * LD, :], block, NT)
                at = pos[t, r : r + 1, :]
                parts.append(jnp.sum(jnp.where(i128 == at, s, 0.0), axis=0, keepdims=True))
            sc = jnp.concatenate(parts, axis=0)
            hi = sc.astype(BF).astype(F32)
            rest = sc - hi
            mid = rest.astype(BF).astype(F32)
            low = rest - mid
            stack = jnp.concatenate(
                [v[:, 128 * i : 128 * i + 128] for v in (hi, mid, low) for i in range(4)], axis=0
            ).astype(BF)
            sums = dot(stack, same, NN)
            total = sums[0:32] + sums[32:64] + sums[64:96]
            score = jnp.concatenate([total[8 * i : 8 * i + 8] for i in range(4)], axis=1)
            slope = (jax.nn.sigmoid(score * (1.0 / math.sqrt(QT * DIM))) - labs[t]).astype(BF).astype(F32)
            for r in range(DB):
                sl = jnp.broadcast_to(slope[r : r + 1], (16, QTOK)).astype(BF)
                at = jnp.broadcast_to(pos[t, r : r + 1, :], (16, QTOK)).astype(F32).astype(BF)
                for i in range(LD // 16):
                    here = (i16 + 16 * i).astype(F32).astype(BF)
                    row = r * LD + i * 16
                    w[row : row + 16, :] = jnp.where(at == here, sl, jnp.zeros_like(sl))
            weights = w[...]
            qacc[rel] += dot(docs_t[...], weights, NN)
            dacc[...] += dot(weights, block, NN)
            return 0

        lax.fori_loop(0, KQ, per_k, 0)
        dgrad[pl.ds(c * DB, DB)] = dacc[...].astype(BF).reshape(DB, LD, DIM)
        return 0

    lax.fori_loop(0, NLOC, per_c, 0)
    near[...] = qacc[0:8].astype(BF)
    far[...] = qacc[8:16].astype(BF)

    for yr in range(4):
        for i in range(2 * CAP):
            j = source[yr * 2 * CAP + i]
            rows = dgrad[jnp.maximum(j, 0)]
            outs[yr][i] = jnp.where(j >= 0, rows, jnp.zeros_like(rows))


def tile_work(place, cand, owners, docs, pos, lab, qs):
    vmem = pl.BlockSpec(memory_space=pltpu.VMEM)
    smem = pl.BlockSpec(memory_space=pltpu.SMEM)
    hbm = pl.BlockSpec(memory_space=pl.ANY)
    half = jax.ShapeDtypeStruct((8, DIM, QTOK), BF)
    slots = jax.ShapeDtypeStruct((2 * CAP, LD, DIM), BF)
    return pl.pallas_call(
        tile_body,
        in_specs=[smem, smem, smem, vmem, vmem, vmem] + [hbm] * 16,
        out_specs=[vmem] * 6,
        out_shape=[half, half] + [slots] * 4,
        scratch_shapes=[
            pltpu.VMEM((16, QTOK, DIM), BF),
            pltpu.VMEM((16, DIM, QTOK), F32),
            pltpu.VMEM((DB * LD, DIM), F32),
            pltpu.VMEM((DIM, DB * LD), BF),
            pltpu.VMEM((NLOC * KQ, DB, QTOK), F32),
            pltpu.VMEM((DB * LD, QTOK), BF),
            pltpu.VMEM((NLOC * DB, LD, DIM), BF),
            pltpu.SMEM((N_ENC * CAP,), jnp.int32),
            pltpu.SemaphoreType.DMA((16,)),
        ],
        compiler_params=pltpu.CompilerParams(vmem_limit_bytes=56 * 2**20),
    )(place, cand, owners, docs, pos, lab, *qs)


def wide(*values):
    total = values[0].astype(F32)
    for v in values[1:]:
        total = total + v.astype(F32)
    return total


def shards(queries, documents, candidates, positions, labels, owner_map, hidden, projection):
    me_blk = lax.axis_index("blk")
    me_enc = lax.axis_index("enc")
    place = jnp.stack([me_blk, me_enc]).astype(jnp.int32)
    own = queries[0]
    pair = [own, shift(own, zl=1)]
    got = {}
    for z in range(2):
        got[0, z, 0] = pair[z]
        for x in (1, 2, 3):
            got[0, z, x] = shift(pair[z], x=-x)
    for z in range(2):
        for x in range(4):
            got[1, z, x] = shift(got[0, z, x], c=1)
    qs = [got[c, z, x] for c in range(2) for z in range(2) for x in range(4)]
    far, near, *slots = tile_work(
        place,
        candidates.reshape(-1),
        owner_map.reshape(-1),
        documents,
        positions.reshape(NLOC * KQ, DB, QTOK),
        labels.reshape(NLOC * KQ * DB, QB),
        qs,
    )
    docs_y = wide(slots[0], *[shift(slots[y], y=y) for y in (1, 2, 3)])
    docs_far = shift(docs_y[CAP:].astype(BF), zh=1)
    grad = (docs_y[:CAP] + docs_far.astype(F32)).astype(BF)
    both = wide(near, shift(far, c=1)).astype(BF).reshape(2, 4, DIM, QTOK)
    q_x = wide(both[:, 0], *[shift(both[:, x], x=x) for x in (1, 2, 3)])
    q_z = q_x[0] + shift(q_x[1].astype(BF), zl=1).astype(F32)
    query_grad = q_z.T[None]

    flat_grad = grad.reshape(-1, DIM)
    flat_hidden = hidden.reshape(-1, hidden.shape[2])
    part = lax.dot_general(flat_hidden, flat_grad, (((0,), (0,)), ((), ())), preferred_element_type=F32)
    hidden_grad = dot(flat_grad, projection, NT).astype(BF).reshape(hidden.shape)

    my_x, my_c = (me_blk // 2) % 4, me_blk % 2
    hid = part.shape[0]
    part = part.reshape(2, 4, hid // 8, DIM)
    give = lax.dynamic_index_in_dim(part, 1 - my_c, 0, False).astype(BF)
    keep = lax.dynamic_index_in_dim(part, my_c, 0, False)
    half = keep + shift(give, c=1).astype(F32)
    half = jnp.roll(half, -my_x, axis=0)
    rest = half.astype(BF)
    quarter = wide(half[0], *[shift(rest[x], x=x) for x in (1, 2, 3)])
    for axis in ("z", "y"):
        mine = quarter.astype(BF)
        if axis == "y":
            a, b, c, d = mine, shift2(mine, y=1), shift2(mine, y=2), shift2(mine, y=3)
        else:
            a, b, c, d = mine, shift2(mine, z=1), shift2(mine, z=2), shift2(mine, z=3)
        quarter = wide(a, b) + wide(c, d)
    mine = quarter.astype(BF)
    line = jnp.stack([mine] + [shift(mine, x=-x) for x in (1, 2, 3)])
    line = jnp.roll(line, my_x, axis=0)
    other = shift(line, c=1)
    weight = jnp.where(my_c == 0, jnp.stack([line, other]), jnp.stack([other, line]))
    weight_grad = weight.astype(F32).reshape(hid, DIM)
    return (query_grad, hidden_grad, weight_grad)


def shift2(value, y=0, z=0):
    pairs = []
    for i in range(N_BLK * N_ENC):
        a, b, d, e, f = coords(i)
        pairs.append((i, number(a ^ (z & 1), b, d, e ^ y, f ^ (z >> 1))))
    return lax.ppermute(value, BOTH, pairs)


def solution(mesh):
    return jax.shard_map(
        shards,
        mesh=mesh,
        in_specs=(
            P(("blk", "enc"), None, None),
            P("blk", None, None),
            P("blk", "enc", None),
            P("blk", "enc", None, None, None),
            P("blk", "enc", None, None, None),
            P("blk", None),
            P(("blk", "enc"), None, None),
            P(),
        ),
        out_specs=(P(("blk", "enc"), None, None), P(("blk", "enc"), None, None), P()),
        check_vma=False,
    )
```

```python
import functools
import math

import jax
import jax.numpy as jnp
from jax import lax
from jax.experimental import pallas as pl
from jax.experimental.pallas import tpu as pltpu
from jax.sharding import PartitionSpec as P

DIM = 128
QT = 32
LD = 128
DB = 8
KQ = 8
QB = 16
QTOK = 512
CAP = 8
NLOC = 4
N_BLK = 16
N_ENC = 8
BF = jnp.bfloat16
F32 = jnp.float32
NN = (((1,), (0,)), ((), ()))
NT = (((1,), (1,)), ((), ()))
BOTH = ("blk", "enc")


def coords(i):
    blk, enc = divmod(i, N_ENC)
    return blk >> 3, (blk >> 1) & 3, blk & 1, enc >> 1, enc & 1


def number(zl, x, c, y, zh):
    return (zl * 8 + x * 2 + c) * N_ENC + y * 2 + zh


def shift(value, zl=0, x=0, c=0, y=0, zh=0):
    pairs = []
    for i in range(N_BLK * N_ENC):
        a, b, d, e, f = coords(i)
        pairs.append((i, number(a ^ zl, (b + x) % 4, d ^ c, (e + y) % 4, f ^ zh)))
    return lax.ppermute(value, BOTH, pairs)


def dot(a, b, dims):
    return lax.dot_general(a, b, dims, preferred_element_type=F32)


def select_body(docs, pos, sel, docs_t):
    n = pos.shape[0]
    step = pl.program_id(0)

    @pl.when(step % (KQ // n) == 0)
    def _():
        for r in range(DB):
            docs_t[r] = docs[0, r * LD : (r + 1) * LD, :].T

    rows = lax.broadcasted_iota(jnp.int32, (16, QTOK), 0)
    for j in range(n):
        for r in range(DB):
            at = jnp.broadcast_to(pos[j, r : r + 1, :], (16, QTOK)).astype(F32).astype(BF)
            hot = jnp.concatenate(
                [
                    jnp.where(at == (rows + 16 * g).astype(F32).astype(BF), jnp.ones_like(at), jnp.zeros_like(at))
                    for g in range(LD // 16)
                ],
                axis=0,
            )
            sel[j, r] = dot(docs_t[r], hot, NN).astype(BF)


def select(docs, pos, n=4):
    per = KQ // n
    return pl.pallas_call(
        select_body,
        grid=(NLOC * KQ // n,),
        in_specs=[
            pl.BlockSpec((1, DB * LD, DIM), lambda s: (s // per, 0, 0)),
            pl.BlockSpec((n, DB, QTOK), lambda s: (s, 0, 0)),
        ],
        out_specs=pl.BlockSpec((n, DB, DIM, QTOK), lambda s: (s, 0, 0, 0)),
        out_shape=jax.ShapeDtypeStruct((NLOC * KQ, DB, DIM, QTOK), BF),
        scratch_shapes=[pltpu.VMEM((DB, DIM, LD), BF)],
        compiler_params=pltpu.CompilerParams(vmem_limit_bytes=40 * 2**20),
    )(docs, pos)


def tile_body(cand, owners, pos, lab, sel, *refs):
    pairs = refs[:8]
    qgrad = refs[8]
    ys = refs[9:13]
    zs = refs[13:15]
    q, qacc, dacc, labs, w, dgrad, source, sems = refs[15:]
    n = sel.shape[0]
    step = pl.program_id(0)
    steps = NLOC * KQ // n
    per = KQ // n
    blk, enc = lax.axis_index("blk"), lax.axis_index("enc")
    my_zl, my_x, my_c = blk // 8, (blk // 2) % 4, blk % 2
    my_y, my_zh = enc // 2, enc % 2

    @pl.when(step == 0)
    def _():
        copies = [pltpu.make_async_copy(pairs[i], q.at[pl.ds(2 * i, 2)], sems.at[i]) for i in range(8)]
        for copy in copies:
            copy.start()
        qacc[...] = jnp.zeros_like(qacc)

        def clear(i, _):
            source[i] = -1
            return 0

        lax.fori_loop(0, N_ENC * CAP, clear, 0)

        def slot_of(i, _):
            o = owners[i, 0]
            row = (((o // 2) - my_y + 4) % 4) * 2 + (o % 2 + my_zh) % 2

            def count(j, m):
                return m + jnp.where(owners[j, 0] == o, 1, 0)

            rank = lax.fori_loop(0, i, count, 0)
            source[row * CAP + rank] = i
            return 0

        lax.fori_loop(0, NLOC * DB, slot_of, 0)
        spread = (
            lax.broadcasted_iota(jnp.int32, (QB, QTOK), 0)
            == lax.broadcasted_iota(jnp.int32, (QB, QTOK), 1) // QT
        ).astype(BF)
        labs[...] = dot(lab[...].astype(BF), spread, NN).reshape(labs.shape)
        for copy in copies:
            copy.wait()

    @pl.when(step % per == 0)
    def _():
        dacc[...] = jnp.zeros_like(dacc)

    rows = lax.broadcasted_iota(jnp.int32, (16, QTOK), 0)
    same = (
        lax.broadcasted_iota(jnp.int32, (128, 128), 0) // QT
        == lax.broadcasted_iota(jnp.int32, (128, 128), 1) // QT
    ).astype(BF)
    for j in range(n):
        t = step * n + j
        g = cand[t // KQ, 0, t % KQ]
        home = (g // 2) % 4 * 4 + g // 8 * 2 + g % 2
        rel = ((g + my_c) % 2) * 8 + ((g // 2) % 4 - my_x + 4) % 4 * 2 + (g // 8 + my_zl) % 2
        parts = [jnp.zeros((8, QTOK), F32) for _ in range(DB)]
        for i in range(DIM // 16):
            block = q[rel, 16 * i : 16 * i + 16, :].astype(F32)
            for r in range(DB):
                prod = sel[j, r, 16 * i : 16 * i + 16, :].astype(F32) * block
                parts[r] = parts[r] + (prod[0:8] + prod[8:16])
        sc = jnp.concatenate([jnp.sum(v, axis=0, keepdims=True) for v in parts], axis=0)
        hi = sc.astype(BF).astype(F32)
        rest = sc - hi
        mid = rest.astype(BF).astype(F32)
        low = rest - mid
        stack = jnp.concatenate(
            [v[:, 128 * i : 128 * i + 128] for v in (hi, mid, low) for i in range(4)], axis=0
        ).astype(BF)
        sums = dot(stack, same, NN)
        total = sums[0:32] + sums[32:64] + sums[64:96]
        score = jnp.concatenate([total[8 * i : 8 * i + 8] for i in range(4)], axis=1)
        slope = (jax.nn.sigmoid(score * (1.0 / math.sqrt(QT * DIM))) - labs[t]).astype(BF).astype(F32)
        for r in range(DB):
            sl = jnp.broadcast_to(slope[r : r + 1], (16, QTOK)).astype(BF)
            at = jnp.broadcast_to(pos[t, r : r + 1, :], (16, QTOK)).astype(F32).astype(BF)
            for i in range(LD // 16):
                here = (rows + 16 * i).astype(F32).astype(BF)
                row = r * LD + i * 16
                w[j, row : row + 16, :] = jnp.where(at == here, sl, jnp.zeros_like(sl))
        dacc[...] += dot(w[j], q[rel], NT)
        for h in range(4):
            lanes = slice(128 * h, 128 * h + 128)
            wide_slope = [jnp.broadcast_to(slope[r : r + 1, lanes], (16, 128)) for r in range(DB)]
            for i in range(DIM // 16):
                span = slice(16 * i, 16 * i + 16)
                acc = qacc[home, span, lanes]
                for r in range(DB):
                    acc = acc + sel[j, r, span, lanes].astype(F32) * wide_slope[r]
                qacc[home, span, lanes] = acc

    @pl.when(step % per == per - 1)
    def _():
        dgrad[pl.ds((step // per) * DB, DB)] = dacc[...].astype(BF).reshape(DB, LD, DIM)

    @pl.when(step == steps - 1)
    def _():
        qgrad[...] = qacc[...].astype(BF)
        for yr in range(4):
            for zr in range(2):
                for s in range(CAP):
                    i = source[(yr * 2 + zr) * CAP + s]
                    doc = dgrad[jnp.maximum(i, 0)]
                    doc = jnp.where(i >= 0, doc, jnp.zeros_like(doc))
                    if s < CAP // 2:
                        ys[yr][zr, s] = doc
                    else:
                        zs[zr][yr, s - CAP // 2] = doc


def tile_work(cand, owners, pos, lab, sel, pairs, n=2):
    vmem = pl.BlockSpec(memory_space=pltpu.VMEM)
    smem = pl.BlockSpec(memory_space=pltpu.SMEM)
    hbm = pl.BlockSpec(memory_space=pl.ANY)
    return pl.pallas_call(
        tile_body,
        grid=(NLOC * KQ // n,),
        in_specs=[smem, smem, vmem, vmem, pl.BlockSpec((n, DB, DIM, QTOK), lambda s: (s, 0, 0, 0))]
        + [hbm] * 8,
        out_specs=[vmem] * 7,
        out_shape=[jax.ShapeDtypeStruct((N_BLK, DIM, QTOK), BF)]
        + [jax.ShapeDtypeStruct((2, CAP // 2, LD, DIM), BF)] * 4
        + [jax.ShapeDtypeStruct((4, CAP // 2, LD, DIM), BF)] * 2,
        scratch_shapes=[
            pltpu.VMEM((16, DIM, QTOK), BF),
            pltpu.VMEM((16, DIM, QTOK), F32),
            pltpu.VMEM((DB * LD, DIM), F32),
            pltpu.VMEM((NLOC * KQ, DB, QTOK), F32),
            pltpu.VMEM((n, DB * LD, QTOK), BF),
            pltpu.VMEM((NLOC * DB, LD, DIM), BF),
            pltpu.SMEM((N_ENC * CAP,), jnp.int32),
            pltpu.SemaphoreType.DMA((8,)),
        ],
        compiler_params=pltpu.CompilerParams(vmem_limit_bytes=56 * 2**20),
    )(cand, owners, pos, lab, sel, *pairs)


def wide(*values):
    total = values[0].astype(F32)
    for v in values[1:]:
        total = total + v.astype(F32)
    return total


def butterfly(value, first, second):
    pairs = []
    for i in range(N_BLK * N_ENC):
        zl, x, c, y, zh = coords(i)
        my, mx, mz = (first, second)[c]
        pairs.append((i, number(zl ^ (mz & 1), x ^ mx, c, y ^ my, zh ^ (mz >> 1))))
    low = lax.reduce_precision(value, 8, 7)
    return low + lax.ppermute(low.astype(BF), BOTH, pairs).astype(F32)


def shards(queries, documents, candidates, positions, labels, owner_map, hidden, projection):
    me_blk = lax.axis_index("blk")
    pos = positions.reshape(NLOC * KQ, DB, QTOK)
    own = queries[0].T
    pair = jnp.stack([own, shift(own, zl=1)])
    line = [pair] + [shift(pair, x=-x) for x in (1, 2, 3)]
    line[1:], sel = lax.optimization_barrier((line[1:], select(documents, pos)))
    pairs = line + [shift(v, c=1) for v in line]
    q_terms, y0, y1, y2, y3, z0, z1 = tile_work(
        candidates,
        owner_map,
        pos,
        labels.reshape(NLOC * KQ * DB, QB),
        sel,
        pairs,
    )
    ry = [shift(y1, y=1), shift(y2, y=2), shift(y3, y=3)]
    rz = shift(z1, zh=1)
    lines = [[z * 8 + x * 2 + c for x in range(4)] for z in range(2) for c in range(2)]
    q_got = lax.all_to_all(
        q_terms.reshape(4, 2, 2, DIM, QTOK), "blk", 0, 0, axis_index_groups=lines
    )
    sum_y = wide(y0, *ry)
    sum_z = wide(z0, rz)
    low_in = shift(sum_y[1].astype(BF), zh=1)
    high_in = [shift(sum_z[y].astype(BF), y=y) for y in (1, 2, 3)]
    low = sum_y[0] + low_in.astype(F32)
    high = sum_z[0] + wide(*high_in)
    grad = jnp.concatenate([low, high], axis=0).astype(BF)

    flat_grad = grad.reshape(-1, DIM)
    flat_hidden = hidden.reshape(-1, hidden.shape[2])
    part = lax.dot_general(flat_hidden, flat_grad, (((0,), (0,)), ((), ())), preferred_element_type=F32)
    hidden_grad = dot(flat_grad, projection, NT).astype(BF).reshape(hidden.shape)

    hid = part.shape[0]
    my_c, my_zl = me_blk % 2, me_blk // 8
    upper, lower = part[: hid // 2], part[hid // 2 :]
    give = jnp.where(my_c == 0, lower, upper).astype(BF)
    keep = jnp.where(my_c == 0, upper, lower)
    half = keep + shift(give, c=1).astype(F32)
    y1, y3, z1, z3, x1, x3 = (1, 0, 0), (3, 0, 0), (0, 0, 1), (0, 0, 3), (0, 1, 0), (0, 3, 0)
    half = butterfly(half, y1, z1)
    half = butterfly(half, y3, z3)
    half, q_got = lax.optimization_barrier((half, q_got))
    q_x = jnp.sum(q_got.astype(F32), axis=0)
    q_core = shift(jnp.where(my_c == 0, q_x[:, 1], q_x[:, 0]).astype(BF), c=1)
    half = butterfly(half, z1, y1)
    half = butterfly(half, z3, y3)
    half, q_core = lax.optimization_barrier((half, q_core))
    q_c = jnp.where(my_c == 0, q_x[:, 0], q_x[:, 1]) + q_core.astype(F32)
    q_far = shift(jnp.where(my_zl == 0, q_c[1], q_c[0]).astype(BF), zl=1)
    half = butterfly(half, x1, x1)
    half, q_far = lax.optimization_barrier((half, q_far))
    query_grad = (jnp.where(my_zl == 0, q_c[0], q_c[1]) + q_far.astype(F32)).T[None]
    half = butterfly(half, x3, x3)
    mine = half.astype(BF)
    other = shift(mine, c=1)
    weight = jnp.where(my_c == 0, jnp.stack([mine, other]), jnp.stack([other, mine]))
    weight_grad = weight.astype(F32).reshape(hid, DIM)
    return (query_grad, hidden_grad, weight_grad)


def solution(mesh):
    return jax.shard_map(
        shards,
        mesh=mesh,
        in_specs=(
            P(("blk", "enc"), None, None),
            P("blk", None, None),
            P("blk", "enc", None),
            P("blk", "enc", None, None, None),
            P("blk", "enc", None, None, None),
            P("blk", None),
            P(("blk", "enc"), None, None),
            P(),
        ),
        out_specs=(P(("blk", "enc"), None, None), P(("blk", "enc"), None, None), P()),
        check_vma=False,
    )
```

```python
import functools
import math

import jax
import jax.numpy as jnp
from jax import lax
from jax.experimental import pallas as pl
from jax.experimental.pallas import tpu as pltpu
from jax.sharding import PartitionSpec as P

DIM = 128
QT = 32
LD = 128
DB = 8
KQ = 8
QB = 16
QTOK = 512
CAP = 8
NLOC = 4
N_BLK = 16
N_ENC = 8
BF = jnp.bfloat16
F32 = jnp.float32
NN = (((1,), (0,)), ((), ()))
NT = (((1,), (1,)), ((), ()))
BOTH = ("blk", "enc")


def coords(i):
    blk, enc = divmod(i, N_ENC)
    return blk >> 3, (blk >> 1) & 3, blk & 1, enc >> 1, enc & 1


def number(zl, x, c, y, zh):
    return (zl * 8 + x * 2 + c) * N_ENC + y * 2 + zh


def shift(value, zl=0, x=0, c=0, y=0, zh=0):
    pairs = []
    for i in range(N_BLK * N_ENC):
        a, b, d, e, f = coords(i)
        pairs.append((i, number(a ^ zl, (b + x) % 4, d ^ c, (e + y) % 4, f ^ zh)))
    return lax.ppermute(value, BOTH, pairs)


def dot(a, b, dims):
    return lax.dot_general(a, b, dims, preferred_element_type=F32)


def select_body(docs, pos, sel, docs_t):
    n = pos.shape[0]
    step = pl.program_id(0)

    @pl.when(step % (KQ // n) == 0)
    def _():
        for r in range(DB):
            docs_t[r] = docs[0, r * LD : (r + 1) * LD, :].T

    rows = lax.broadcasted_iota(jnp.int32, (16, QTOK), 0)
    for j in range(n):
        for r in range(DB):
            at = jnp.broadcast_to(pos[j, r : r + 1, :], (16, QTOK)).astype(F32).astype(BF)
            hot = jnp.concatenate(
                [
                    jnp.where(at == (rows + 16 * g).astype(F32).astype(BF), jnp.ones_like(at), jnp.zeros_like(at))
                    for g in range(LD // 16)
                ],
                axis=0,
            )
            sel[j, r] = dot(docs_t[r], hot, NN).astype(BF)


def select(docs, pos, n=4):
    per = KQ // n
    return pl.pallas_call(
        select_body,
        grid=(NLOC * KQ // n,),
        in_specs=[
            pl.BlockSpec((1, DB * LD, DIM), lambda s: (s // per, 0, 0)),
            pl.BlockSpec((n, DB, QTOK), lambda s: (s, 0, 0)),
        ],
        out_specs=pl.BlockSpec((n, DB, DIM, QTOK), lambda s: (s, 0, 0, 0)),
        out_shape=jax.ShapeDtypeStruct((NLOC * KQ, DB, DIM, QTOK), BF),
        scratch_shapes=[pltpu.VMEM((DB, DIM, LD), BF)],
        compiler_params=pltpu.CompilerParams(vmem_limit_bytes=40 * 2**20),
    )(docs, pos)


def tile_body(cand, owners, pos, lab, sel, *refs):
    pairs = refs[:8]
    qgrad = refs[8]
    ys = refs[9:13]
    zs = refs[13:15]
    q, qacc, dacc, labs, w, slopes, blocks, dgrad, source, used, sems = refs[15:]
    n = sel.shape[0]
    step = pl.program_id(0)
    steps = NLOC * KQ // n
    per = KQ // n
    blk, enc = lax.axis_index("blk"), lax.axis_index("enc")
    my_zl, my_x, my_c = blk // 8, (blk // 2) % 4, blk % 2
    my_y, my_zh = enc // 2, enc % 2

    @pl.when(step == 0)
    def _():
        copies = [pltpu.make_async_copy(pairs[i], q.at[pl.ds(2 * i, 2)], sems.at[i]) for i in range(8)]
        for copy in copies:
            copy.start()
        qacc[...] = jnp.zeros_like(qacc)

        def clear(i, _):
            source[i] = -1
            return 0

        lax.fori_loop(0, N_ENC * CAP, clear, 0)
        for o in range(N_ENC):
            used[o] = 0

        def slot_of(i, _):
            o = owners[i, 0]
            row = (((o // 2) - my_y + 4) % 4) * 2 + (o % 2 + my_zh) % 2
            rank = used[o]
            used[o] = rank + 1
            source[row * CAP + rank] = i
            return 0

        lax.fori_loop(0, NLOC * DB, slot_of, 0)
        spread = (
            lax.broadcasted_iota(jnp.int32, (QB, QTOK), 0)
            == lax.broadcasted_iota(jnp.int32, (QB, QTOK), 1) // QT
        ).astype(BF)
        labs[...] = dot(lab[...].astype(BF), spread, NN).reshape(labs.shape)
        for copy in copies:
            copy.wait()

    @pl.when(step % per == 0)
    def _():
        dacc[...] = jnp.zeros_like(dacc)

    rows = lax.broadcasted_iota(jnp.int32, (16, QTOK), 0)
    same = (
        lax.broadcasted_iota(jnp.int32, (128, 128), 0) // QT
        == lax.broadcasted_iota(jnp.int32, (128, 128), 1) // QT
    ).astype(BF)
    def block_of(j):
        t = step * n + j
        g = cand[t // KQ, 0, t % KQ]
        home = (g // 2) % 4 * 4 + g // 8 * 2 + g % 2
        rel = ((g + my_c) % 2) * 8 + ((g // 2) % 4 - my_x + 4) % 4 * 2 + (g // 8 + my_zl) % 2
        return home, rel

    def score_tile(j, _):
        rel = block_of(j)[1]
        parts = [jnp.zeros((8, QTOK), F32) for _ in range(DB)]
        for i in range(DIM // 16):
            block = q[rel, 16 * i : 16 * i + 16, :].astype(F32)
            for r in range(DB):
                prod = sel[j, r, 16 * i : 16 * i + 16, :].astype(F32) * block
                parts[r] = parts[r] + (prod[0:8] + prod[8:16])
        for r in range(DB):
            slopes[j, r : r + 1, :] = jnp.sum(parts[r], axis=0, keepdims=True)
        return 0

    lax.fori_loop(0, n, score_tile, 0)
    sc = slopes[...].reshape(n * DB, QTOK)
    hi = sc.astype(BF).astype(F32)
    rest = sc - hi
    mid = rest.astype(BF).astype(F32)
    low = rest - mid
    stack = jnp.concatenate(
        [v[:, 128 * i : 128 * i + 128] for v in (hi, mid, low) for i in range(4)], axis=0
    ).astype(BF)
    sums = dot(stack, same, NN)
    m = 4 * n * DB
    total = sums[0:m] + sums[m : 2 * m] + sums[2 * m : 3 * m]
    score = jnp.concatenate([total[n * DB * i : n * DB * (i + 1)] for i in range(4)], axis=1)
    marks = labs[pl.ds(step * n, n)].reshape(n * DB, QTOK)
    slope = (jax.nn.sigmoid(score * (1.0 / math.sqrt(QT * DIM))) - marks).astype(BF).astype(F32)
    slopes[...] = slope.reshape(n, DB, QTOK)
    for j in range(n):
        blocks[:, j * QTOK : (j + 1) * QTOK] = q[block_of(j)[1]]
    for r in range(DB):
        for j in range(n):
            sl = jnp.broadcast_to(slopes[j, r : r + 1], (16, QTOK)).astype(BF)
            at = jnp.broadcast_to(pos[step * n + j, r : r + 1, :], (16, QTOK)).astype(F32).astype(BF)
            for i in range(LD // 16):
                here = (rows + 16 * i).astype(F32).astype(BF)
                row = r * LD + i * 16
                w[row : row + 16, j * QTOK : (j + 1) * QTOK] = jnp.where(at == here, sl, jnp.zeros_like(sl))
    dacc[...] += dot(w[...], blocks[...], NT)

    def query_tile(j, _):
        home = block_of(j)[0]
        for h in range(4):
            lanes = slice(128 * h, 128 * h + 128)
            wide_slope = [jnp.broadcast_to(slopes[j, r : r + 1, lanes], (16, 128)) for r in range(DB)]
            for i in range(DIM // 16):
                span = slice(16 * i, 16 * i + 16)
                acc = qacc[home, span, lanes]
                for r in range(DB):
                    acc = acc + sel[j, r, span, lanes].astype(F32) * wide_slope[r]
                qacc[home, span, lanes] = acc
        return 0

    lax.fori_loop(0, n, query_tile, 0)

    @pl.when(step % per == per - 1)
    def _():
        dgrad[pl.ds((step // per) * DB, DB)] = dacc[...].astype(BF).reshape(DB, LD, DIM)

    @pl.when(step == steps - 1)
    def _():
        qgrad[...] = qacc[...].astype(BF)
        for yr in range(4):
            for zr in range(2):
                for s in range(CAP):
                    i = source[(yr * 2 + zr) * CAP + s]
                    doc = dgrad[jnp.maximum(i, 0)]
                    doc = jnp.where(i >= 0, doc, jnp.zeros_like(doc))
                    if s < CAP // 2:
                        ys[yr][zr, s] = doc
                    else:
                        zs[zr][yr, s - CAP // 2] = doc


def tile_work(cand, owners, pos, lab, sel, pairs, n=4):
    vmem = pl.BlockSpec(memory_space=pltpu.VMEM)
    smem = pl.BlockSpec(memory_space=pltpu.SMEM)
    hbm = pl.BlockSpec(memory_space=pl.ANY)
    return pl.pallas_call(
        tile_body,
        grid=(NLOC * KQ // n,),
        in_specs=[smem, smem, vmem, vmem, pl.BlockSpec((n, DB, DIM, QTOK), lambda s: (s, 0, 0, 0))]
        + [hbm] * 8,
        out_specs=[vmem] * 7,
        out_shape=[jax.ShapeDtypeStruct((N_BLK, DIM, QTOK), BF)]
        + [jax.ShapeDtypeStruct((2, CAP // 2, LD, DIM), BF)] * 4
        + [jax.ShapeDtypeStruct((4, CAP // 2, LD, DIM), BF)] * 2,
        scratch_shapes=[
            pltpu.VMEM((16, DIM, QTOK), BF),
            pltpu.VMEM((16, DIM, QTOK), F32),
            pltpu.VMEM((DB * LD, DIM), F32),
            pltpu.VMEM((NLOC * KQ, DB, QTOK), F32),
            pltpu.VMEM((DB * LD, n * QTOK), BF),
            pltpu.VMEM((n, DB, QTOK), F32),
            pltpu.VMEM((DIM, n * QTOK), BF),
            pltpu.VMEM((NLOC * DB, LD, DIM), BF),
            pltpu.SMEM((N_ENC * CAP,), jnp.int32),
            pltpu.SMEM((N_ENC,), jnp.int32),
            pltpu.SemaphoreType.DMA((8,)),
        ],
        compiler_params=pltpu.CompilerParams(vmem_limit_bytes=56 * 2**20),
    )(cand, owners, pos, lab, sel, *pairs)


def wide(*values):
    total = values[0].astype(F32)
    for v in values[1:]:
        total = total + v.astype(F32)
    return total


def butterfly(value, first, second):
    pairs = []
    for i in range(N_BLK * N_ENC):
        zl, x, c, y, zh = coords(i)
        my, mx, mz = (first, second)[c]
        pairs.append((i, number(zl ^ (mz & 1), x ^ mx, c, y ^ my, zh ^ (mz >> 1))))
    low = lax.reduce_precision(value, 8, 7)
    return low + lax.ppermute(low.astype(BF), BOTH, pairs).astype(F32)


def shards(queries, documents, candidates, positions, labels, owner_map, hidden, projection):
    me_blk = lax.axis_index("blk")
    pos = positions.reshape(NLOC * KQ, DB, QTOK)
    own = queries[0].T
    pair = jnp.stack([own, shift(own, zl=1)])
    line = [pair] + [shift(pair, x=-x) for x in (1, 2, 3)]
    line[1:], sel = lax.optimization_barrier((line[1:], select(documents, pos)))
    pairs = line + [shift(v, c=1) for v in line]
    q_terms, y0, y1, y2, y3, z0, z1 = tile_work(
        candidates,
        owner_map,
        pos,
        labels.reshape(NLOC * KQ * DB, QB),
        sel,
        pairs,
    )
    ry = [shift(y1, y=1), shift(y2, y=2), shift(y3, y=3)]
    rz = shift(z1, zh=1)
    lines = [[z * 8 + x * 2 + c for x in range(4)] for z in range(2) for c in range(2)]
    q_got = lax.all_to_all(
        q_terms.reshape(4, 2, 2, DIM, QTOK), "blk", 0, 0, axis_index_groups=lines
    )
    sum_y = wide(y0, *ry)
    sum_z = wide(z0, rz)
    low_in = shift(sum_y[1].astype(BF), zh=1)
    high_in = [shift(sum_z[y].astype(BF), y=y) for y in (1, 2, 3)]
    low = sum_y[0] + low_in.astype(F32)
    high = sum_z[0] + wide(*high_in)
    grad = jnp.concatenate([low, high], axis=0).astype(BF)

    flat_grad = grad.reshape(-1, DIM)
    flat_hidden = hidden.reshape(-1, hidden.shape[2])
    part = lax.dot_general(flat_hidden, flat_grad, (((0,), (0,)), ((), ())), preferred_element_type=F32)
    hidden_grad = dot(flat_grad, projection, NT).astype(BF).reshape(hidden.shape)

    hid = part.shape[0]
    my_c, my_zl = me_blk % 2, me_blk // 8
    upper, lower = part[: hid // 2], part[hid // 2 :]
    give = jnp.where(my_c == 0, lower, upper).astype(BF)
    keep = jnp.where(my_c == 0, upper, lower)
    half = keep + shift(give, c=1).astype(F32)
    y1, y3, z1, z3, x1, x3 = (1, 0, 0), (3, 0, 0), (0, 0, 1), (0, 0, 3), (0, 1, 0), (0, 3, 0)
    half = butterfly(half, y1, z1)
    half = butterfly(half, y3, z3)
    half, q_got = lax.optimization_barrier((half, q_got))
    q_x = jnp.sum(q_got.astype(F32), axis=0)
    q_core = shift(jnp.where(my_c == 0, q_x[:, 1], q_x[:, 0]).astype(BF), c=1)
    half = butterfly(half, z1, y1)
    half = butterfly(half, z3, y3)
    half, q_core = lax.optimization_barrier((half, q_core))
    q_c = jnp.where(my_c == 0, q_x[:, 0], q_x[:, 1]) + q_core.astype(F32)
    q_far = shift(jnp.where(my_zl == 0, q_c[1], q_c[0]).astype(BF), zl=1)
    half = butterfly(half, x1, x1)
    half, q_far = lax.optimization_barrier((half, q_far))
    query_grad = (jnp.where(my_zl == 0, q_c[0], q_c[1]) + q_far.astype(F32)).T[None]
    half = butterfly(half, x3, x3)
    mine = half.astype(BF)
    other = shift(mine, c=1)
    weight = jnp.where(my_c == 0, jnp.stack([mine, other]), jnp.stack([other, mine]))
    weight_grad = weight.astype(F32).reshape(hid, DIM)
    return (query_grad, hidden_grad, weight_grad)


def solution(mesh):
    return jax.shard_map(
        shards,
        mesh=mesh,
        in_specs=(
            P(("blk", "enc"), None, None),
            P("blk", None, None),
            P("blk", "enc", None),
            P("blk", "enc", None, None, None),
            P("blk", "enc", None, None, None),
            P("blk", None),
            P(("blk", "enc"), None, None),
            P(),
        ),
        out_specs=(P(("blk", "enc"), None, None), P(("blk", "enc"), None, None), P()),
        check_vma=False,
    )
```

```python
import functools
import math

import jax
import jax.numpy as jnp
from jax import lax
from jax.experimental import pallas as pl
from jax.experimental.pallas import tpu as pltpu
from jax.sharding import PartitionSpec as P

DIM = 128
QT = 32
LD = 128
DB = 8
KQ = 8
QB = 16
QTOK = 512
CAP = 8
NLOC = 4
N_BLK = 16
N_ENC = 8
BF = jnp.bfloat16
F32 = jnp.float32
NN = (((1,), (0,)), ((), ()))
NT = (((1,), (1,)), ((), ()))
BOTH = ("blk", "enc")


def coords(i):
    blk, enc = divmod(i, N_ENC)
    return blk >> 3, (blk >> 1) & 3, blk & 1, enc >> 1, enc & 1


def number(zl, x, c, y, zh):
    return (zl * 8 + x * 2 + c) * N_ENC + y * 2 + zh


def shift(value, zl=0, x=0, c=0, y=0, zh=0):
    pairs = []
    for i in range(N_BLK * N_ENC):
        a, b, d, e, f = coords(i)
        pairs.append((i, number(a ^ zl, (b + x) % 4, d ^ c, (e + y) % 4, f ^ zh)))
    return lax.ppermute(value, BOTH, pairs)


def dot(a, b, dims):
    return lax.dot_general(a, b, dims, preferred_element_type=F32)


def select_body(docs, pos, sel, docs_t):
    n = pos.shape[0]
    step = pl.program_id(0)

    @pl.when(step % (KQ // n) == 0)
    def _():
        for r in range(DB):
            docs_t[r] = docs[0, r * LD : (r + 1) * LD, :].T

    rows = lax.broadcasted_iota(jnp.int32, (16, QTOK), 0)
    for j in range(n):
        for r in range(DB):
            at = jnp.broadcast_to(pos[j, r : r + 1, :], (16, QTOK)).astype(F32).astype(BF)
            hot = jnp.concatenate(
                [
                    jnp.where(at == (rows + 16 * g).astype(F32).astype(BF), jnp.ones_like(at), jnp.zeros_like(at))
                    for g in range(LD // 16)
                ],
                axis=0,
            )
            sel[j, r] = dot(docs_t[r], hot, NN).astype(BF)


def select(docs, pos, n=4):
    per = KQ // n
    return pl.pallas_call(
        select_body,
        grid=(NLOC * KQ // n,),
        in_specs=[
            pl.BlockSpec((1, DB * LD, DIM), lambda s: (s // per, 0, 0)),
            pl.BlockSpec((n, DB, QTOK), lambda s: (s, 0, 0)),
        ],
        out_specs=pl.BlockSpec((n, DB, DIM, QTOK), lambda s: (s, 0, 0, 0)),
        out_shape=jax.ShapeDtypeStruct((NLOC * KQ, DB, DIM, QTOK), BF),
        scratch_shapes=[pltpu.VMEM((DB, DIM, LD), BF)],
        compiler_params=pltpu.CompilerParams(vmem_limit_bytes=40 * 2**20),
    )(docs, pos)


def tile_body(cand, owners, pos, lab, sel, *refs):
    pairs = refs[:8]
    qgrad = refs[8]
    ys = refs[9:13]
    zs = refs[13:15]
    q, qacc, dacc, labs, w, slopes, blocks, dgrad, source, used, sems = refs[15:]
    n = sel.shape[0]
    step = pl.program_id(0)
    steps = NLOC * KQ // n
    per = KQ // n
    blk, enc = lax.axis_index("blk"), lax.axis_index("enc")
    my_zl, my_x, my_c = blk // 8, (blk // 2) % 4, blk % 2
    my_y, my_zh = enc // 2, enc % 2

    @pl.when(step == 0)
    def _():
        copies = [pltpu.make_async_copy(pairs[i], q.at[pl.ds(2 * i, 2)], sems.at[i]) for i in range(8)]
        for copy in copies:
            copy.start()
        qacc[...] = jnp.zeros_like(qacc)

        def clear(i, _):
            source[i] = -1
            return 0

        lax.fori_loop(0, N_ENC * CAP, clear, 0)
        for o in range(N_ENC):
            used[o] = 0

        def slot_of(i, _):
            o = owners[i, 0]
            row = (((o // 2) - my_y + 4) % 4) * 2 + (o % 2 + my_zh) % 2
            rank = used[o]
            used[o] = rank + 1
            source[row * CAP + rank] = i
            return 0

        lax.fori_loop(0, NLOC * DB, slot_of, 0)
        spread = (
            lax.broadcasted_iota(jnp.int32, (QB, QTOK), 0)
            == lax.broadcasted_iota(jnp.int32, (QB, QTOK), 1) // QT
        ).astype(BF)
        labs[...] = dot(lab[...].astype(BF), spread, NN).reshape(labs.shape)
        for copy in copies:
            copy.wait()

    @pl.when(step % per == 0)
    def _():
        dacc[...] = jnp.zeros_like(dacc)

    rows = lax.broadcasted_iota(jnp.int32, (16, QTOK), 0)
    same = (
        lax.broadcasted_iota(jnp.int32, (128, 128), 0) // QT
        == lax.broadcasted_iota(jnp.int32, (128, 128), 1) // QT
    ).astype(BF)
    def block_of(j):
        t = step * n + j
        g = cand[t // KQ, 0, t % KQ]
        home = (g // 2) % 4 * 4 + g // 8 * 2 + g % 2
        rel = ((g + my_c) % 2) * 8 + ((g // 2) % 4 - my_x + 4) % 4 * 2 + (g // 8 + my_zl) % 2
        return home, rel

    def score_tile(j, _):
        rel = block_of(j)[1]
        parts = [jnp.zeros((8, QTOK), F32) for _ in range(DB)]
        for i in range(DIM // 16):
            block = q[rel, 16 * i : 16 * i + 16, :].astype(F32)
            for r in range(DB):
                prod = sel[j, r, 16 * i : 16 * i + 16, :].astype(F32) * block
                parts[r] = parts[r] + (prod[0:8] + prod[8:16])
        for r in range(DB):
            slopes[j, r : r + 1, :] = jnp.sum(parts[r], axis=0, keepdims=True)
        return 0

    lax.fori_loop(0, n, score_tile, 0)
    sc = slopes[...].reshape(n * DB, QTOK)
    hi = sc.astype(BF).astype(F32)
    rest = sc - hi
    mid = rest.astype(BF).astype(F32)
    low = rest - mid
    stack = jnp.concatenate(
        [v[:, 128 * i : 128 * i + 128] for v in (hi, mid, low) for i in range(4)], axis=0
    ).astype(BF)
    sums = dot(stack, same, NN)
    m = 4 * n * DB
    total = sums[0:m] + sums[m : 2 * m] + sums[2 * m : 3 * m]
    score = jnp.concatenate([total[n * DB * i : n * DB * (i + 1)] for i in range(4)], axis=1)
    marks = labs[pl.ds(step * n, n)].reshape(n * DB, QTOK)
    slope = (jax.nn.sigmoid(score * (1.0 / math.sqrt(QT * DIM))) - marks).astype(BF).astype(F32)
    slopes[...] = slope.reshape(n, DB, QTOK)
    for j in range(n):
        blocks[:, j * QTOK : (j + 1) * QTOK] = q[block_of(j)[1]]
    for r in range(DB):
        for j in range(n):
            sl = jnp.broadcast_to(slopes[j, r : r + 1], (16, QTOK)).astype(BF)
            at = jnp.broadcast_to(pos[step * n + j, r : r + 1, :], (16, QTOK)).astype(F32).astype(BF)
            for i in range(LD // 16):
                here = (rows + 16 * i).astype(F32).astype(BF)
                row = r * LD + i * 16
                w[row : row + 16, j * QTOK : (j + 1) * QTOK] = jnp.where(at == here, sl, jnp.zeros_like(sl))
    dacc[...] += dot(w[...], blocks[...], NT)

    def query_tile(j, _):
        home = block_of(j)[0]
        for h in range(4):
            lanes = slice(128 * h, 128 * h + 128)
            wide_slope = [jnp.broadcast_to(slopes[j, r : r + 1, lanes], (16, 128)) for r in range(DB)]
            for i in range(DIM // 16):
                span = slice(16 * i, 16 * i + 16)
                acc = qacc[home, span, lanes]
                for r in range(DB):
                    acc = acc + sel[j, r, span, lanes].astype(F32) * wide_slope[r]
                qacc[home, span, lanes] = acc
        return 0

    lax.fori_loop(0, n, query_tile, 0)

    @pl.when(step % per == per - 1)
    def _():
        dgrad[pl.ds((step // per) * DB, DB)] = dacc[...].astype(BF).reshape(DB, LD, DIM)

    @pl.when(step == steps - 1)
    def _():
        qgrad[...] = qacc[...].astype(BF)
        for yr in range(4):
            for zr in range(2):
                for s in range(CAP):
                    i = source[(yr * 2 + zr) * CAP + s]
                    doc = dgrad[jnp.maximum(i, 0)]
                    doc = jnp.where(i >= 0, doc, jnp.zeros_like(doc))
                    if s < CAP // 2:
                        ys[yr][zr, s] = doc
                    else:
                        zs[zr][yr, s - CAP // 2] = doc


def tile_work(cand, owners, pos, lab, sel, pairs, n=4):
    vmem = pl.BlockSpec(memory_space=pltpu.VMEM)
    smem = pl.BlockSpec(memory_space=pltpu.SMEM)
    hbm = pl.BlockSpec(memory_space=pl.ANY)
    return pl.pallas_call(
        tile_body,
        grid=(NLOC * KQ // n,),
        in_specs=[smem, smem, vmem, vmem, pl.BlockSpec((n, DB, DIM, QTOK), lambda s: (s, 0, 0, 0))]
        + [hbm] * 8,
        out_specs=[vmem] * 7,
        out_shape=[jax.ShapeDtypeStruct((N_BLK, DIM, QTOK), BF)]
        + [jax.ShapeDtypeStruct((2, CAP // 2, LD, DIM), BF)] * 4
        + [jax.ShapeDtypeStruct((4, CAP // 2, LD, DIM), BF)] * 2,
        scratch_shapes=[
            pltpu.VMEM((16, DIM, QTOK), BF),
            pltpu.VMEM((16, DIM, QTOK), F32),
            pltpu.VMEM((DB * LD, DIM), F32),
            pltpu.VMEM((NLOC * KQ, DB, QTOK), F32),
            pltpu.VMEM((DB * LD, n * QTOK), BF),
            pltpu.VMEM((n, DB, QTOK), F32),
            pltpu.VMEM((DIM, n * QTOK), BF),
            pltpu.VMEM((NLOC * DB, LD, DIM), BF),
            pltpu.SMEM((N_ENC * CAP,), jnp.int32),
            pltpu.SMEM((N_ENC,), jnp.int32),
            pltpu.SemaphoreType.DMA((8,)),
        ],
        compiler_params=pltpu.CompilerParams(vmem_limit_bytes=56 * 2**20),
    )(cand, owners, pos, lab, sel, *pairs)


def wide(*values):
    total = values[0].astype(F32)
    for v in values[1:]:
        total = total + v.astype(F32)
    return total


def butterfly(value, first, second):
    pairs = []
    for i in range(N_BLK * N_ENC):
        zl, x, c, y, zh = coords(i)
        my, mx, mz = (first, second)[c]
        pairs.append((i, number(zl ^ (mz & 1), x ^ mx, c, y ^ my, zh ^ (mz >> 1))))
    low = lax.reduce_precision(value, 8, 7)
    return low + lax.ppermute(low.astype(BF), BOTH, pairs).astype(F32)


def shards(queries, documents, candidates, positions, labels, owner_map, hidden, projection):
    me_blk = lax.axis_index("blk")
    pos = positions.reshape(NLOC * KQ, DB, QTOK)
    own = queries[0].T
    pair = jnp.stack([own, shift(own, zl=1)])
    line = [pair] + [shift(pair, x=-x) for x in (1, 2, 3)]
    line[1:], sel = lax.optimization_barrier((line[1:], select(documents, pos)))
    pairs = line + [shift(v, c=1) for v in line]
    q_terms, y0, y1, y2, y3, z0, z1 = tile_work(
        candidates,
        owner_map,
        pos,
        labels.reshape(NLOC * KQ * DB, QB),
        sel,
        pairs,
    )
    ry = [shift(y1, y=1), shift(y2, y=2), shift(y3, y=3)]
    rz = shift(z1, zh=1)
    lines = [[z * 8 + x * 2 + c for x in range(4)] for z in range(2) for c in range(2)]
    q_got = lax.all_to_all(
        q_terms.reshape(4, 2, 2, DIM, QTOK), "blk", 0, 0, axis_index_groups=lines
    )
    sum_y = wide(y0, *ry)
    sum_z = wide(z0, rz)
    low_in = shift(sum_y[1].astype(BF), zh=1)
    high_in = [shift(sum_z[y].astype(BF), y=y) for y in (1, 2, 3)]
    low = sum_y[0] + low_in.astype(F32)
    high = sum_z[0] + wide(*high_in)
    grad = jnp.concatenate([low, high], axis=0).astype(BF)

    flat_grad = grad.reshape(-1, DIM)
    flat_hidden = hidden.reshape(-1, hidden.shape[2])
    part = lax.dot_general(flat_hidden, flat_grad, (((0,), (0,)), ((), ())), preferred_element_type=F32)
    hidden_grad = dot(flat_grad, projection, NT).astype(BF).reshape(hidden.shape)

    hid = part.shape[0]
    my_c, my_zl = me_blk % 2, me_blk // 8
    upper, lower = part[: hid // 2], part[hid // 2 :]
    give = jnp.where(my_c == 0, lower, upper).astype(BF)
    keep = jnp.where(my_c == 0, upper, lower)
    half = keep + shift(give, c=1).astype(F32)
    y1, y3, z1, z3, x1, x3 = (1, 0, 0), (3, 0, 0), (0, 0, 1), (0, 0, 3), (0, 1, 0), (0, 3, 0)
    half = butterfly(half, y1, z1)
    half = butterfly(half, y3, z3)
    half, q_got = lax.optimization_barrier((half, q_got))
    q_x = jnp.sum(q_got.astype(F32), axis=0)
    q_core = shift(jnp.where(my_c == 0, q_x[:, 1], q_x[:, 0]).astype(BF), c=1)
    half = butterfly(half, z1, x1)
    half = butterfly(half, z3, x3)
    half, q_core = lax.optimization_barrier((half, q_core))
    q_c = jnp.where(my_c == 0, q_x[:, 0], q_x[:, 1]) + q_core.astype(F32)
    q_far = shift(jnp.where(my_zl == 0, q_c[1], q_c[0]).astype(BF), zl=1)
    half = butterfly(half, x1, y1)
    half, q_far = lax.optimization_barrier((half, q_far))
    query_grad = (jnp.where(my_zl == 0, q_c[0], q_c[1]) + q_far.astype(F32)).T[None]
    half = butterfly(half, x3, y3)
    mine = half.astype(BF)
    other = shift(mine, c=1)
    weight = jnp.where(my_c == 0, jnp.stack([mine, other]), jnp.stack([other, mine]))
    weight_grad = weight.astype(F32).reshape(hid, DIM)
    return (query_grad, hidden_grad, weight_grad)


def solution(mesh):
    return jax.shard_map(
        shards,
        mesh=mesh,
        in_specs=(
            P(("blk", "enc"), None, None),
            P("blk", None, None),
            P("blk", "enc", None),
            P("blk", "enc", None, None, None),
            P("blk", "enc", None, None, None),
            P("blk", None),
            P(("blk", "enc"), None, None),
            P(),
        ),
        out_specs=(P(("blk", "enc"), None, None), P(("blk", "enc"), None, None), P()),
        check_vma=False,
    )
```
